32 devices in a mesh: member: 2 (over y), patch: 4 (over x, core), chan: 4 (over z).
Axes of the slice: x: 2, y: 2, z: 4, core: 2. Of those that a mesh axis runs over, the one named last changes fastest.
Arguments:
- grid_latent: bfloat16 [1024, 8192], P('member', 'patch'), parts along dimension 0, may hold values from -6 to 6
- mesh_latent: bfloat16 [1024, 6144], P('member', 'patch'), parts along dimension 0, may hold values from -6 to 6
- edge_sender: int32 [4, 4, 1024], P('patch'), may hold values from 0 to 2047
- edge_receiver: int32 [4, 4, 1024], P(None, 'patch'), may hold values from 0 to 1535
- edge_count: int32 [4, 4], replicated, may hold values from 0 to 1024, as said below
- nbr_index: int32 [16, 6144], P(None, 'patch'), may hold values from 0 to 1791, as said below
- halo_send: int32 [4, 2, 128], P('patch'), may hold values from 0 to 1535
- w_edge_send: bfloat16 [512, 512], P(None, 'chan'), may hold values from -0.25 to 0.25
- w_edge_recv: bfloat16 [512, 512], P(None, 'chan'), may hold values from -0.25 to 0.25
- b_edge: float32 [512], P('chan'), may hold values from -4 to 4
- w_edge_out: bfloat16 [512, 512], P('chan'), may hold values from -0.125 to 0.125
- ln_gain: float32 [512], replicated, may hold values from 0.5 to 1.5
- w_query: bfloat16 [512, 512], replicated, may hold values from -1 to 1
- w_key: bfloat16 [512, 512], replicated, may hold values from -1 to 1
- w_value: bfloat16 [512, 512], P(None, 'chan'), may hold values from -0.25 to 0.25
- w_attn_out: bfloat16 [512, 512], P('chan'), may hold values from -0.25 to 0.25
Outputs:
- mesh_out: bfloat16 [1024, 6144], P('member', 'patch'), parts along dimension 0
The draws below stay inside these ranges and needn't reach their ends.
There are 2 independent parts, one for each index of `member`. The reference program is written for one: setup_inputs(seed, part) draws one part's arguments, and reference() takes and returns one part's arrays. A program takes and returns all parts, laid end to end along the dimension named above; an argument that names none is the same for every part. Nothing has to cross between parts.
Inputs may be any that keep to these rules, and one draw needn't show every extreme that they name: edge_sender[b, p, c] is a row among band b's 2048 grid points; only slots c < edge_count[b, p] hold edges. edge_receiver[b, p, c] is a node among patch p's 1536 mesh nodes. edge_count[b, p] edges go from band b to patch p; in every draw some patch receives 1024 from every band. `nbr_index`: read as in the neighbour step. halo_send[p, 0] are the nodes of patch p offered to the patch before it, halo_send[p, 1] those offered to the patch after it.
All inputs are finite; a program needn't handle non-finite values.
Results may differ from the reference program's by a relative error of at most 0.0072.
Values may be sent and summed in bfloat16 or wider, within the bound.
A program may use at most 128 MiB of HBM per device.

```python
import jax
import jax.numpy as jnp
from jax import lax

D = 512
H = 512
HEADS = 4
K = 16
GRID_DEV = 2048
MESH_DEV = 1536
CAP = 1024
HALO = 128
PATCHES = 4
GRID = 8192
MESH = 6144
N_PATCH = 4


def draw_w_query(key, part):
    key = jax.random.fold_in(key, 3)
    private = jax.random.normal(key, (D, D), jnp.float32) * D ** (-0.5)
    result = private
    return jnp.clip(result, -1.0, 1.0).astype(jnp.bfloat16)


def draw_w_key(key, part):
    key = jax.random.fold_in(key, 4)
    private = jax.random.normal(key, (D, D), jnp.float32) * D ** (-0.5)
    result = private
    return jnp.clip(result, -1.0, 1.0).astype(jnp.bfloat16)


def draw_edge_count(key, part):
    key = jax.random.fold_in(key, 5)
    key_counts, key_busy = jax.random.split(key)
    counts = jax.random.randint(key_counts, (N_PATCH, N_PATCH), 0, 3 * CAP // 4 + 1)
    busiest = jax.random.randint(key_busy, (), 0, N_PATCH)
    column_ids = jnp.arange(N_PATCH, dtype=jnp.int32)[None, :]
    return jnp.where(column_ids == busiest, CAP, counts).astype(jnp.int32)


def draw_nbr_index(key, part):
    key = jax.random.fold_in(key, 7)
    key_offset, key_halo, key_remote, key_self = jax.random.split(key, 4)
    own_row = (jnp.arange(MESH, dtype=jnp.int32) % MESH_DEV)[None, :]
    offset = jax.random.randint(key_offset, (K, MESH), -48, 49)
    nearby = (own_row + offset) % MESH_DEV
    halo_pick = jax.random.randint(key_halo, (K, MESH), MESH_DEV, MESH_DEV + 2 * HALO)
    remote = jax.random.randint(key_remote, (K, MESH), 0, 4) == 0
    picked = jnp.where(remote, halo_pick, nearby)
    self_slot = jax.random.randint(key_self, (1, MESH), 0, 2) == 0
    first_slot = jnp.where(self_slot, own_row, picked[:1])
    return jnp.concatenate([first_slot, picked[1:]], axis=0).astype(jnp.int32)


def plant(drawn, own_key, low, top_value):
    longest = drawn.shape.index(max(drawn.shape))
    spots = []
    for shift in (0, 1):
        where = [jax.random.randint(jax.random.fold_in(own_key, axis), (), 0, length) for axis, length in enumerate(drawn.shape)]
        where[longest] = (where[longest] + shift) % drawn.shape[longest]
        spots.append(tuple(where))
    return drawn.at[spots[0]].set(low).at[spots[1]].set(top_value)


def block_levels(own_key, dims, cuts, least, high):
    factor_of = 1.0
    for axis_at, shards_of in cuts:
        steps = jax.random.uniform(jax.random.fold_in(jax.random.fold_in(own_key, 6), axis_at), (shards_of,), jnp.float32, least / len(cuts), high / len(cuts))
        factor_of = factor_of * jnp.repeat(jnp.exp(steps), dims[axis_at] // shards_of).reshape((-1,) + (1,) * (len(dims) - 1 - axis_at))
    return factor_of


def noise(key, shape, scale, bound, cuts=(), kind=jnp.bfloat16):
    level = block_levels(key, shape, cuts, -0.22, 0.18) if cuts else 1.0
    drawn = jax.random.normal(key, shape, jnp.float32) * scale * level
    return jnp.minimum(jnp.maximum(drawn, -bound), bound).astype(kind)


def setup_inputs(seed: int = 0, part: int = 0) -> dict:
    arg_keys = jax.random.split(jax.random.key(seed), 17)
    own_keys = jax.random.split(jax.random.fold_in(arg_keys[16], part), 17)
    return {
        "grid_latent": noise(own_keys[0], (D, GRID), 1.0, 6.0, ((1, 4),)),
        "mesh_latent": noise(own_keys[1], (D, MESH), 1.0, 6.0, ((1, 4),)),
        "edge_sender": plant(jax.random.randint(arg_keys[2], (PATCHES, PATCHES, CAP), 0, GRID_DEV), jax.random.fold_in(arg_keys[2], 1), 0, GRID_DEV - 1).astype(jnp.int32),
        "edge_receiver": plant(jax.random.randint(arg_keys[3], (PATCHES, PATCHES, CAP), 0, MESH_DEV), jax.random.fold_in(arg_keys[3], 1), 0, MESH_DEV - 1).astype(jnp.int32),
        "edge_count": draw_edge_count(jax.random.fold_in(arg_keys[16], 71), part),
        "nbr_index": draw_nbr_index(jax.random.fold_in(arg_keys[16], 71), part),
        "halo_send": plant(jax.random.randint(arg_keys[6], (PATCHES, 2, HALO), 0, MESH_DEV), jax.random.fold_in(arg_keys[6], 1), 0, MESH_DEV - 1).astype(jnp.int32),
        "w_edge_send": noise(arg_keys[7], (D, H), D ** -0.5, 0.25, ((1, 4),)),
        "w_edge_recv": noise(arg_keys[8], (D, H), D ** -0.5, 0.25, ((1, 4),)),
        "b_edge": noise(arg_keys[9], (H,), 1.0, 4.0, ((0, 4),), jnp.float32),
        "w_edge_out": noise(arg_keys[10], (H, D), (4 * H) ** -0.5, 0.125, ((0, 4),)),
        "ln_gain": jnp.clip(1.0 + 0.1 * jax.random.normal(arg_keys[11], (D,), jnp.float32), 0.5, 1.5),
        "w_query": draw_w_query(jax.random.fold_in(arg_keys[16], 71), part),
        "w_key": draw_w_key(jax.random.fold_in(arg_keys[16], 71), part),
        "w_value": noise(arg_keys[14], (D, D), D ** -0.5, 0.25, ((1, 4),)),
        "w_attn_out": noise(arg_keys[15], (D, D), D ** -0.5, 0.25, ((0, 4),)),
    }


def layer_norm(encoded, ln_gain):
    average = lax.optimization_barrier(jnp.mean(encoded, axis=0, keepdims=True))
    centred = encoded - average
    variance = lax.optimization_barrier(jnp.mean(centred * centred, axis=0, keepdims=True))
    return (centred * lax.rsqrt(variance + 1e-05) * ln_gain[:, None]).astype(jnp.bfloat16)

def reference(grid_latent, mesh_latent, edge_sender, edge_receiver, edge_count, nbr_index, halo_send, w_edge_send, w_edge_recv, b_edge, w_edge_out, ln_gain, w_query, w_key, w_value, w_attn_out):
    sender_proj = jnp.dot(w_edge_send.T, grid_latent, preferred_element_type=jnp.float32).astype(jnp.bfloat16)
    recv_proj = jnp.dot(w_edge_recv.T, mesh_latent, preferred_element_type=jnp.float32).astype(jnp.bfloat16)
    band_ids = jnp.arange(N_PATCH, dtype=jnp.int32)
    slot_ids = jnp.arange(CAP, dtype=jnp.int32)

    def add_band(node_acc, inputs):
        band_index, senders, receivers, counts = inputs
        source = (band_index * GRID_DEV + senders).reshape(-1).astype(jnp.int32)
        target = (band_ids[:, None] * MESH_DEV + receivers).reshape(-1).astype(jnp.int32)
        usable = (slot_ids[None, :] < counts[:, None]).reshape(-1)
        summed = jnp.take(sender_proj, source, axis=1).astype(jnp.float32) + jnp.take(recv_proj, target, axis=1).astype(jnp.float32) + b_edge[:, None]
        hidden = jnp.where(usable[None, :], jax.nn.silu(summed), 0.0).astype(jnp.bfloat16)
        return (node_acc.at[:, target].add(hidden.astype(jnp.float32)), None)
    node_acc, leftover = lax.scan(add_band, jnp.zeros((H, MESH), jnp.float32), (band_ids, edge_sender, edge_receiver, edge_count))
    node_sum = node_acc.astype(jnp.bfloat16)
    encoded = mesh_latent.astype(jnp.float32) + jnp.dot(w_edge_out.T, node_sum, preferred_element_type=jnp.float32)
    normed = layer_norm(encoded, ln_gain)
    query_rows = jnp.dot(w_query.T, normed, preferred_element_type=jnp.float32).astype(jnp.bfloat16)
    key_rows = jnp.dot(w_key.T, normed, preferred_element_type=jnp.float32).astype(jnp.bfloat16)
    value_rows = jnp.dot(w_value.T, normed, preferred_element_type=jnp.float32).astype(jnp.bfloat16)
    column_patch = jnp.arange(MESH, dtype=jnp.int32) // MESH_DEV
    lower_patch = ((column_patch - 1) % N_PATCH)[None, :]
    upper_patch = ((column_patch + 1) % N_PATCH)[None, :]
    from_lower = lower_patch * MESH_DEV + halo_send[lower_patch, 1, jnp.clip(nbr_index - MESH_DEV, 0, HALO - 1)]
    from_upper = upper_patch * MESH_DEV + halo_send[upper_patch, 0, jnp.clip(nbr_index - MESH_DEV - HALO, 0, HALO - 1)]
    neighbour = jnp.where(nbr_index < MESH_DEV, column_patch[None, :] * MESH_DEV + nbr_index, jnp.where(nbr_index < MESH_DEV + HALO, from_lower, from_upper)).astype(jnp.int32)
    head_size = D // HEADS
    block_rows = 512 if MESH_DEV % 512 == 0 else MESH_DEV

    def attend(first_row):
        query_block = lax.dynamic_slice_in_dim(query_rows, first_row, block_rows, 1).astype(jnp.float32).reshape(HEADS, head_size, block_rows)
        chosen = lax.dynamic_slice_in_dim(neighbour, first_row, block_rows, 1).reshape(-1)
        key_block = jnp.take(key_rows, chosen, axis=1).astype(jnp.float32).reshape(HEADS, head_size, K, block_rows)
        value_block = jnp.take(value_rows, chosen, axis=1).astype(jnp.float32).reshape(HEADS, head_size, K, block_rows)
        scores = jnp.einsum('hdb,hdkb->hkb', query_block, key_block) * head_size ** (-0.5)
        weights = jax.nn.softmax(scores, axis=1).astype(jnp.bfloat16)
        blended = jnp.einsum('hkb,hdkb->hdb', weights.astype(jnp.float32), value_block)
        return blended.reshape(D, block_rows).astype(jnp.bfloat16)
    blocks = lax.map(attend, jnp.arange(MESH // block_rows, dtype=jnp.int32) * block_rows)
    blended = jnp.transpose(blocks, (1, 0, 2)).reshape(D, MESH)
    mesh_out = encoded + jnp.dot(w_attn_out.T, blended, preferred_element_type=jnp.float32)
    return mesh_out.astype(jnp.bfloat16)
```

```python
import functools

import jax
import jax.numpy as jnp
from jax import lax
from jax.experimental import pallas as pl
from jax.experimental.pallas import tpu as pltpu
from jax.sharding import PartitionSpec as P

HEADS = 4
BF16 = jnp.bfloat16
F32 = jnp.float32
VMEM = pltpu.VMEM
QUERY_BLOCK = 256
NODE_BLOCK = 512
ONEHOT_ROWS = 256


def contract0(weight, operand):
    return lax.dot_general(
        weight, operand, (((0,), (0,)), ((), ())), preferred_element_type=F32
    )


def one_hot(first, rows, index_row):
    shape = (rows, index_row.shape[1])
    ids = lax.broadcasted_iota(jnp.int32, shape, 0)
    return jnp.where(ids == index_row - first, 1.0, 0.0).astype(BF16)


def call(body, out_shape, flops, nbytes, **kw):
    return pl.pallas_call(
        body,
        out_shape=out_shape,
        compiler_params=pltpu.CompilerParams(vmem_limit_bytes=40 * 2**20),
        cost_estimate=pl.CostEstimate(
            flops=int(flops), bytes_accessed=int(nbytes), transcendentals=0
        ),
        **kw,
    )


def pick_columns(table_ref, index_row):
    picked = None
    for first in range(0, table_ref.shape[1], ONEHOT_ROWS):
        term = jnp.dot(
            table_ref[:, first : first + ONEHOT_ROWS],
            one_hot(first, ONEHOT_ROWS, index_row),
            preferred_element_type=F32,
        )
        picked = term if picked is None else picked + term
    return picked


def project_and_pick(latent_ref, weight_ref, index_ref, out_ref, table_ref):
    @pl.when(pl.program_id(0) == 0)
    def _():
        table_ref[...] = contract0(weight_ref[...], latent_ref[...]).astype(BF16)

    index_row = index_ref[pl.ds(pl.program_id(0), 1), :]
    out_ref[0] = pick_columns(table_ref, index_row).astype(BF16)


def project_pick(latent, weight, index):
    blocks, cap = index.shape
    depth, width = weight.shape
    nodes = latent.shape[1]
    whole = lambda shape: pl.BlockSpec(shape, lambda j: (0,) * len(shape))
    return call(
        project_and_pick,
        jax.ShapeDtypeStruct((blocks, width, cap), BF16),
        2 * width * nodes * (depth + blocks * cap),
        2 * (latent.size + weight.size + blocks * width * cap),
        grid=(blocks,),
        in_specs=[whole(latent.shape), whole(weight.shape), whole(index.shape)],
        out_specs=pl.BlockSpec((1, width, cap), lambda j: (j, 0, 0)),
        scratch_shapes=[VMEM((width, nodes), BF16)],
    )(latent, weight, index)


def edge_sum_kernel(sent_ref, received_ref, bias_ref, index_ref, out_ref, acc_ref):
    step = pl.program_id(0)
    summed = sent_ref[0].astype(F32) + received_ref[0].astype(F32) + bias_ref[...]
    hidden = (summed / (1.0 + jnp.exp(-summed))).astype(BF16)
    index_row = index_ref[pl.ds(step, 1), :]
    nodes = acc_ref.shape[1]

    @pl.when(step == 0)
    def _():
        acc_ref[...] = jnp.zeros_like(acc_ref)

    for first in range(0, nodes, ONEHOT_ROWS):
        acc_ref[:, first : first + ONEHOT_ROWS] += lax.dot_general(
            hidden,
            one_hot(first, ONEHOT_ROWS, index_row),
            (((1,), (1,)), ((), ())),
            preferred_element_type=F32,
        )

    @pl.when(step == pl.num_programs(0) - 1)
    def _():
        out_ref[...] = acc_ref[...].astype(BF16)


def edge_sum(sent, received, bias, index, nodes):
    blocks, width, cap = sent.shape
    whole = lambda shape: pl.BlockSpec(shape, lambda j: (0,) * len(shape))
    block = pl.BlockSpec((1, width, cap), lambda j: (j, 0, 0))
    return call(
        edge_sum_kernel,
        jax.ShapeDtypeStruct((width, nodes), BF16),
        2 * width * nodes * blocks * cap,
        4 * sent.size,
        grid=(blocks,),
        in_specs=[block, block, whole(bias.shape), whole(index.shape)],
        out_specs=whole((width, nodes)),
        scratch_shapes=[VMEM((width, nodes), F32)],
    )(sent, received, bias, index)


def count_kernel(index_ref, out_ref):
    index = index_ref[...]
    slots, width = index.shape
    rows = 64
    ids = lax.broadcasted_iota(jnp.int32, (rows, width), 0)

    def body(step, carry):
        first = step * rows
        here = ids + first
        total = jnp.zeros((rows, width), F32)
        for slot in range(slots):
            total += jnp.where(here == index[slot : slot + 1, :], 1.0, 0.0)
        out_ref[pl.ds(pl.multiple_of(first, rows), rows), :] = total.astype(BF16)
        return carry

    lax.fori_loop(0, out_ref.shape[0] // rows, body, 0)


def count_slots(nbr_index, table_rows):
    slots, nodes = nbr_index.shape
    return call(
        count_kernel,
        jax.ShapeDtypeStruct((table_rows, nodes), BF16),
        40e9,
        2 * table_rows * nodes,
        grid=(nodes // QUERY_BLOCK,),
        in_specs=[pl.BlockSpec((slots, QUERY_BLOCK), lambda j: (0, j))],
        out_specs=pl.BlockSpec((table_rows, QUERY_BLOCK), lambda j: (0, j)),
    )(nbr_index)


def encode_kernel(
    head_size, mesh_ref, sum_ref, w_out_ref, gain_ref, w_query_ref, w_key_ref, w_value_ref,
    offer_ref, encoded_ref, query_ref, key_value_ref, offered_ref, acc_ref,
):
    step = pl.program_id(0)
    width = w_value_ref.shape[1]
    head = lax.axis_index("chan") * width // head_size
    columns = pl.ds(pl.multiple_of(head * head_size, head_size), head_size)
    encoded = mesh_ref[...].astype(F32) + contract0(w_out_ref[...], sum_ref[...])
    encoded_ref[...] = encoded
    average = jnp.mean(encoded, axis=0, keepdims=True)
    centred = encoded - average
    variance = jnp.mean(centred * centred, axis=0, keepdims=True)
    normed = (centred * lax.rsqrt(variance + 1e-05) * gain_ref[...]).astype(BF16)
    query_ref[...] = contract0(w_query_ref[:, columns], normed).astype(BF16)
    key = contract0(w_key_ref[:, columns], normed).astype(BF16)
    value = contract0(w_value_ref[...], normed).astype(BF16)
    key_value_ref[:head_size] = key
    key_value_ref[head_size:] = value
    hot = one_hot(step * NODE_BLOCK, NODE_BLOCK, offer_ref[...])

    @pl.when(step == 0)
    def _():
        acc_ref[...] = jnp.zeros_like(acc_ref)

    acc_ref[:head_size] += jnp.dot(key, hot, preferred_element_type=F32)
    acc_ref[head_size:] += jnp.dot(value, hot, preferred_element_type=F32)

    @pl.when(step == pl.num_programs(0) - 1)
    def _():
        offered_ref[...] = acc_ref[...].astype(BF16)


def encode(mesh_latent, node_sum, w_edge_out, gain, w_query, w_key, w_value, offer):
    model_width, nodes = mesh_latent.shape
    hidden = node_sum.shape[0]
    width = w_value.shape[1]
    head_size = model_width // HEADS
    both = head_size + width
    offers = offer.shape[1]
    whole = lambda shape: pl.BlockSpec(shape, lambda j: (0,) * len(shape))
    block = lambda rows: pl.BlockSpec((rows, NODE_BLOCK), lambda j: (0, j))
    return call(
        functools.partial(encode_kernel, head_size),
        [
            jax.ShapeDtypeStruct((model_width, nodes), F32),
            jax.ShapeDtypeStruct((head_size, nodes), BF16),
            jax.ShapeDtypeStruct((both, nodes), BF16),
            jax.ShapeDtypeStruct((both, offers), BF16),
        ],
        2 * model_width * nodes * (hidden + both + head_size),
        10 * mesh_latent.size,
        grid=(nodes // NODE_BLOCK,),
        in_specs=[
            block(model_width),
            block(hidden),
            whole(w_edge_out.shape),
            whole(gain.shape),
            whole(w_query.shape),
            whole(w_key.shape),
            whole(w_value.shape),
            whole(offer.shape),
        ],
        out_specs=[block(model_width), block(head_size), block(both), whole((both, offers))],
        scratch_shapes=[VMEM((both, offers), F32)],
    )(mesh_latent, node_sum, w_edge_out, gain, w_query, w_key, w_value, offer)


def attend_kernel(
    query_ref, own_ref, lower_ref, upper_ref, count_ref, out_ref, key_ref, value_ref
):
    head_size = query_ref.shape[0]

    @pl.when(pl.program_id(0) == 0)
    def _():
        first = 0
        for part in (own_ref, lower_ref, upper_ref):
            rows = part.shape[1]
            key_ref[first : first + rows, :] = part[:head_size].T
            value_ref[:, first : first + rows] = part[head_size:]
            first += rows

    scores = jnp.dot(key_ref[...], query_ref[...], preferred_element_type=F32)
    scores = scores * (head_size**-0.5)
    count = count_ref[...].astype(F32)
    scores = jnp.where(count > 0.0, scores, -3e38)
    top = jnp.max(scores, axis=0, keepdims=True)
    weight = jnp.where(count > 0.0, jnp.exp(scores - top), 0.0)
    total = jnp.sum(weight * count, axis=0, keepdims=True)
    attention = (weight * (1.0 / total)).astype(BF16) * count_ref[...]
    out_ref[...] = jnp.dot(value_ref[...], attention, preferred_element_type=F32).astype(BF16)


def attend(query, own, lower, upper, count):
    head_size, nodes = query.shape
    width = own.shape[0] - head_size
    rows = count.shape[0]
    whole = lambda shape: pl.BlockSpec(shape, lambda j: (0,) * len(shape))
    block = lambda rows: pl.BlockSpec((rows, QUERY_BLOCK), lambda j: (0, j))
    return call(
        attend_kernel,
        jax.ShapeDtypeStruct((width, nodes), BF16),
        2 * nodes * rows * (head_size + width),
        2 * count.size,
        grid=(nodes // QUERY_BLOCK,),
        in_specs=[
            block(head_size),
            whole(own.shape),
            whole(lower.shape),
            whole(upper.shape),
            block(rows),
        ],
        out_specs=block(width),
        scratch_shapes=[VMEM((rows, head_size), BF16), VMEM((width, rows), BF16)],
    )(query, own, lower, upper, count)


def output_kernel(encoded_ref, blended_ref, weight_ref, out_ref):
    out_ref[...] = (encoded_ref[...] + contract0(weight_ref[...], blended_ref[...])).astype(BF16)


def output(encoded, blended, weight):
    model_width, nodes = encoded.shape
    block = lambda rows: pl.BlockSpec((rows, NODE_BLOCK), lambda j: (0, j))
    return call(
        output_kernel,
        jax.ShapeDtypeStruct((model_width, nodes), BF16),
        2 * weight.size * nodes,
        8 * encoded.size,
        grid=(nodes // NODE_BLOCK,),
        in_specs=[
            block(model_width),
            block(blended.shape[0]),
            pl.BlockSpec(weight.shape, lambda j: (0, 0)),
        ],
        out_specs=block(model_width),
    )(encoded, blended, weight)


def per_device(
    grid_latent,
    mesh_latent,
    edge_sender,
    edge_receiver,
    edge_count,
    nbr_index,
    halo_send,
    w_edge_send,
    w_edge_recv,
    b_edge,
    w_edge_out,
    ln_gain,
    w_query,
    w_key,
    w_value,
    w_attn_out,
):
    patch_pos = lax.axis_index("patch")
    patches = lax.axis_size("patch")
    nodes = mesh_latent.shape[1]
    capacity = edge_sender.shape[2]
    halo_rows = halo_send.shape[2]
    counts_in = jnp.take(edge_count, patch_pos, axis=1)
    usable = jnp.arange(capacity, dtype=jnp.int32)[None, :] < counts_in[:, None]
    target = jnp.where(usable, edge_receiver[:, 0, :], -1)

    w_edge_out_all = lax.all_gather(w_edge_out, "chan", axis=0, tiled=True)
    w_attn_out_all = lax.all_gather(w_attn_out, "chan", axis=0, tiled=True)

    outgoing = project_pick(grid_latent, w_edge_send, edge_sender[0])
    sent = lax.all_to_all(outgoing, "patch", split_axis=0, concat_axis=0, tiled=True)
    received = project_pick(mesh_latent, w_edge_recv, target)
    node_sum = edge_sum(sent, received, b_edge[:, None], target, nodes)
    node_sum_all = lax.all_gather(node_sum, "chan", axis=0, tiled=True)
    count = count_slots(nbr_index, nodes + 2 * halo_rows)
    encoded, query, key_value, offered = encode(
        mesh_latent, node_sum_all, w_edge_out_all, ln_gain[:, None],
        w_query, w_key, w_value, halo_send.reshape(1, -1),
    )
    up = [(i, (i + 1) % patches) for i in range(patches)]
    down = [((i + 1) % patches, i) for i in range(patches)]
    lower = lax.ppermute(offered[:, halo_rows:], "patch", up)
    upper = lax.ppermute(offered[:, :halo_rows], "patch", down)
    blended = attend(query, key_value, lower, upper, count)
    blended_all = lax.all_gather(blended, "chan", axis=0, tiled=True)
    return output(encoded, blended_all, w_attn_out_all)


def solution(mesh):
    in_specs = (
        P("member", "patch"),
        P("member", "patch"),
        P("patch", None, None),
        P(None, "patch", None),
        P(),
        P(None, "patch"),
        P("patch", None, None),
        P(None, "chan"),
        P(None, "chan"),
        P("chan"),
        P("chan", None),
        P(),
        P(),
        P(),
        P(None, "chan"),
        P("chan", None),
    )
    out_specs = P("member", "patch")
    return jax.shard_map(
        per_device, mesh=mesh, in_specs=in_specs, out_specs=out_specs, check_vma=False
    )
```

```python
import functools

import jax
import jax.numpy as jnp
from jax import lax
from jax.experimental import pallas as pl
from jax.experimental.pallas import tpu as pltpu
from jax.sharding import PartitionSpec as P

HEADS = 4
BF16 = jnp.bfloat16
F32 = jnp.float32
VMEM = pltpu.VMEM
QUERY_BLOCK = 256
NODE_BLOCK = 512
ONEHOT_ROWS = 256
COUNT_ROWS = 64


def contract0(weight, operand):
    return lax.dot_general(
        weight, operand, (((0,), (0,)), ((), ())), preferred_element_type=F32
    )


def one_hot(first, rows, index_row):
    shape = (rows, index_row.shape[1])
    ids = lax.broadcasted_iota(jnp.int32, shape, 0)
    return jnp.where(ids == index_row - first, 1.0, 0.0).astype(BF16)


def pick_columns(table_ref, index_row):
    picked = None
    for first in range(0, table_ref.shape[1], ONEHOT_ROWS):
        term = jnp.dot(
            table_ref[:, first : first + ONEHOT_ROWS],
            one_hot(first, ONEHOT_ROWS, index_row),
            preferred_element_type=F32,
        )
        picked = term if picked is None else picked + term
    return picked


def kernel(
    patches, chans,
    grid_ref, mesh_ref, sender_ref, target_ref, nbr_ref, offer_ref,
    w_send_ref, w_recv_ref, bias_ref, w_edge_out_ref, gain_ref, w_query_ref, w_key_ref,
    w_value_ref, w_attn_out_ref,
    out_ref,
    sender_table, recv_table, send_buf, recv_buf, received, acc, sums_mine, sums,
    w_edge_out, w_attn_out, encoded, query, key, value, offered_acc, offered, halo, count,
    blended_mine, blended,
    weight_send, weight_recv, edge_send, edge_recv, sum_send, sum_recv, halo_send, halo_recv,
    blend_send, blend_recv,
):
    patch = lax.axis_index("patch")
    chan = lax.axis_index("chan")
    nodes = mesh_ref.shape[1]
    width = w_value_ref.shape[1]
    head_size = query.shape[0]
    node_blocks = nodes // NODE_BLOCK
    query_blocks = nodes // QUERY_BLOCK
    halo_rows = halo.shape[2]

    barrier = pltpu.get_barrier_semaphore()
    for off in range(1, chans):
        pl.semaphore_signal(
            barrier, inc=1, device_id={"chan": lax.rem(chan + off, chans)},
            device_id_type=pl.DeviceIdType.MESH,
        )
    for off in range(1, patches):
        pl.semaphore_signal(
            barrier, inc=1, device_id={"patch": lax.rem(patch + off, patches)},
            device_id_type=pl.DeviceIdType.MESH,
        )
    pl.semaphore_wait(barrier, chans + patches - 2)

    def to_chans(source, target, send_sems, recv_sems):
        return [
            pltpu.make_async_remote_copy(
                src_ref=source, dst_ref=target,
                send_sem=send_sems.at[off - 1], recv_sem=recv_sems.at[off - 1],
                device_id={"chan": lax.rem(chan + off, chans)},
                device_id_type=pl.DeviceIdType.MESH,
            )
            for off in range(1, chans)
        ]

    pending = []

    def start(copies):
        for copy in copies:
            copy.start()
        pending.extend(copies)
        return copies

    edge_out_copies = start(
        to_chans(w_edge_out_ref, w_edge_out.at[chan], weight_send.at[0], weight_recv.at[0])
    )
    w_edge_out[chan] = w_edge_out_ref[...]
    w_attn_out[chan] = w_attn_out_ref[...]

    sender_table[...] = contract0(w_send_ref[...], grid_ref[...]).astype(BF16)
    offs = sorted(range(1, patches), key=lambda off: -min(off, patches - off))
    edge_copies = {}
    for off in offs:
        other = lax.rem(patch + off, patches)
        send_buf[off] = pick_columns(sender_table, sender_ref[pl.ds(other, 1), :]).astype(BF16)
        edge_copies[off] = pltpu.make_async_remote_copy(
            src_ref=send_buf.at[off], dst_ref=recv_buf.at[off],
            send_sem=edge_send.at[off], recv_sem=edge_recv.at[off],
            device_id={"patch": other}, device_id_type=pl.DeviceIdType.MESH,
        )
        start([edge_copies[off]])
    attn_out_copies = start(
        to_chans(w_attn_out_ref, w_attn_out.at[chan], weight_send.at[1], weight_recv.at[1])
    )
    recv_buf[0] = pick_columns(sender_table, sender_ref[pl.ds(patch, 1), :]).astype(BF16)

    recv_table[...] = contract0(w_recv_ref[...], mesh_ref[...]).astype(BF16)
    order = [0] + offs
    for off in order:
        band = lax.rem(patch + patches - off, patches)
        received[off] = pick_columns(recv_table, target_ref[pl.ds(band, 1), :]).astype(BF16)
    for place, off in enumerate(order):
        if off:
            edge_copies[off].wait_recv()
        band = lax.rem(patch + patches - off, patches)
        index_row = target_ref[pl.ds(band, 1), :]
        summed = recv_buf[off].astype(F32) + received[off].astype(F32) + bias_ref[...]
        hidden = (summed / (1.0 + jnp.exp(-summed))).astype(BF16)
        for first in range(0, nodes, ONEHOT_ROWS):
            columns = slice(first, first + ONEHOT_ROWS)
            term = lax.dot_general(
                hidden, one_hot(first, ONEHOT_ROWS, index_row),
                (((1,), (1,)), ((), ())), preferred_element_type=F32,
            )
            if place:
                term += acc[:, columns]
            acc[:, columns] = term

    sum_copies = []
    for block in range(node_blocks):
        node_sum = acc[:, block * NODE_BLOCK : (block + 1) * NODE_BLOCK].astype(BF16)
        sums_mine[block] = node_sum
        sum_copies.append(
            start(
                to_chans(
                    sums_mine.at[block], sums.at[block, chan],
                    sum_send.at[block], sum_recv.at[block],
                )
            )
        )
        sums[block, chan] = node_sum

    def count_block(block):
        index = nbr_ref[:, block * QUERY_BLOCK : (block + 1) * QUERY_BLOCK]
        ids = lax.broadcasted_iota(jnp.int32, (COUNT_ROWS, QUERY_BLOCK), 0)

        def body(step, carry):
            first = step * COUNT_ROWS
            here = ids + first
            total = jnp.zeros((COUNT_ROWS, QUERY_BLOCK), F32)
            for slot in range(index.shape[0]):
                total += jnp.where(here == index[slot : slot + 1, :], 1.0, 0.0)
            rows = pl.ds(pl.multiple_of(first, COUNT_ROWS), COUNT_ROWS)
            count[block, rows, :] = total.astype(BF16)
            return carry

        lax.fori_loop(0, count.shape[1] // COUNT_ROWS, body, 0)

    for block in range(query_blocks - 1):
        count_block(block)

    for copy in edge_out_copies:
        copy.wait_recv()
    head = chan * width // head_size
    columns = pl.ds(pl.multiple_of(head * head_size, head_size), head_size)
    for block in range(node_blocks):
        for copy in sum_copies[block]:
            copy.wait_recv()
        here = slice(block * NODE_BLOCK, (block + 1) * NODE_BLOCK)
        hidden_units = chans * w_edge_out.shape[1]
        weight = w_edge_out[...].reshape(hidden_units, -1)
        node_sum = sums[block].reshape(hidden_units, -1)
        enc = mesh_ref[:, here].astype(F32) + contract0(weight, node_sum)
        encoded[:, here] = enc
        average = jnp.mean(enc, axis=0, keepdims=True)
        centred = enc - average
        variance = jnp.mean(centred * centred, axis=0, keepdims=True)
        normed = (centred * lax.rsqrt(variance + 1e-05) * gain_ref[...]).astype(BF16)
        query[:, here] = contract0(w_query_ref[:, columns], normed).astype(BF16)
        block_key = contract0(w_key_ref[:, columns], normed).astype(BF16)
        block_value = contract0(w_value_ref[...], normed).astype(BF16)
        key[here, :] = block_key.T
        value[:, here] = block_value
        hot = one_hot(block * NODE_BLOCK, NODE_BLOCK, offer_ref[...])
        key_term = jnp.dot(block_key, hot, preferred_element_type=F32)
        value_term = jnp.dot(block_value, hot, preferred_element_type=F32)
        if block:
            key_term += offered_acc[:head_size]
            value_term += offered_acc[head_size:]
        offered_acc[:head_size] = key_term
        offered_acc[head_size:] = value_term

    halo_copies = []
    for side in range(2):
        offered[side] = offered_acc[:, side * halo_rows : (side + 1) * halo_rows].astype(BF16)
        step = 1 if side == 1 else patches - 1
        halo_copies.append(
            pltpu.make_async_remote_copy(
                src_ref=offered.at[side], dst_ref=halo.at[side],
                send_sem=halo_send.at[side], recv_sem=halo_recv.at[side],
                device_id={"patch": lax.rem(patch + step, patches)},
                device_id_type=pl.DeviceIdType.MESH,
            )
        )
    start(halo_copies)
    count_block(query_blocks - 1)
    first = nodes
    for side in (1, 0):
        halo_copies[side].wait_recv()
        key[first : first + halo_rows, :] = halo[side, :head_size].T
        value[:, first : first + halo_rows] = halo[side, head_size:]
        first += halo_rows

    blend_copies = []
    for block in range(query_blocks):
        here = slice(block * QUERY_BLOCK, (block + 1) * QUERY_BLOCK)
        scores = jnp.dot(key[...], query[:, here], preferred_element_type=F32)
        scores = scores * (head_size**-0.5)
        slots = count[block].astype(F32)
        scores = jnp.where(slots > 0.0, scores, -3e38)
        top = jnp.max(scores, axis=0, keepdims=True)
        weight = jnp.where(slots > 0.0, jnp.exp(scores - top), 0.0)
        total = jnp.sum(weight * slots, axis=0, keepdims=True)
        attention = (weight * (1.0 / total)).astype(BF16) * count[block]
        mixed = jnp.dot(value[...], attention, preferred_element_type=F32).astype(BF16)
        blended_mine[block] = mixed
        blend_copies.append(
            start(
                to_chans(
                    blended_mine.at[block], blended.at[block, chan],
                    blend_send.at[block], blend_recv.at[block],
                )
            )
        )
        blended[block, chan] = mixed

    for copy in attn_out_copies:
        copy.wait_recv()
    for block in range(query_blocks):
        for copy in blend_copies[block]:
            copy.wait_recv()
        here = slice(block * QUERY_BLOCK, (block + 1) * QUERY_BLOCK)
        rows = chans * w_attn_out.shape[1]
        weight = w_attn_out[...].reshape(rows, -1)
        update = contract0(weight, blended[block].reshape(rows, -1))
        out_ref[:, here] = (encoded[:, here] + update).astype(BF16)

    for copy in pending:
        copy.wait_send()


def per_device(
    grid_latent,
    mesh_latent,
    edge_sender,
    edge_receiver,
    edge_count,
    nbr_index,
    halo_send,
    w_edge_send,
    w_edge_recv,
    b_edge,
    w_edge_out,
    ln_gain,
    w_query,
    w_key,
    w_value,
    w_attn_out,
):
    patch_pos = lax.axis_index("patch")
    patches = lax.axis_size("patch")
    chans = lax.axis_size("chan")
    model_width, nodes = mesh_latent.shape
    capacity = edge_sender.shape[2]
    halo_rows = halo_send.shape[2]
    hidden = w_edge_send.shape[1]
    width = w_value.shape[1]
    head_size = model_width // HEADS
    both = head_size + width
    table_rows = nodes + 2 * halo_rows
    node_blocks = nodes // NODE_BLOCK
    query_blocks = nodes // QUERY_BLOCK
    counts_in = jnp.take(edge_count, patch_pos, axis=1)
    usable = jnp.arange(capacity, dtype=jnp.int32)[None, :] < counts_in[:, None]
    target = jnp.where(usable, edge_receiver[:, 0, :], -1)
    sem = lambda *shape: pltpu.SemaphoreType.DMA(shape)
    return pl.pallas_call(
        functools.partial(kernel, patches, chans),
        out_shape=jax.ShapeDtypeStruct((model_width, nodes), BF16),
        in_specs=[pl.BlockSpec(memory_space=VMEM)] * 15,
        out_specs=pl.BlockSpec(memory_space=VMEM),
        scratch_shapes=[
            VMEM((hidden, grid_latent.shape[1]), BF16),
            VMEM((hidden, nodes), BF16),
            VMEM((patches, hidden, capacity), BF16),
            VMEM((patches, hidden, capacity), BF16),
            VMEM((patches, hidden, capacity), BF16),
            VMEM((hidden, nodes), F32),
            VMEM((node_blocks, hidden, NODE_BLOCK), BF16),
            VMEM((node_blocks, chans, hidden, NODE_BLOCK), BF16),
            VMEM((chans,) + w_edge_out.shape, BF16),
            VMEM((chans,) + w_attn_out.shape, BF16),
            VMEM((model_width, nodes), F32),
            VMEM((head_size, nodes), BF16),
            VMEM((table_rows, head_size), BF16),
            VMEM((width, table_rows), BF16),
            VMEM((both, 2 * halo_rows), F32),
            VMEM((2, both, halo_rows), BF16),
            VMEM((2, both, halo_rows), BF16),
            VMEM((query_blocks, table_rows, QUERY_BLOCK), BF16),
            VMEM((query_blocks, width, QUERY_BLOCK), BF16),
            VMEM((query_blocks, chans, width, QUERY_BLOCK), BF16),
            sem(2, chans), sem(2, chans),
            sem(patches), sem(patches),
            sem(node_blocks, chans), sem(node_blocks, chans),
            sem(2), sem(2),
            sem(query_blocks, chans), sem(query_blocks, chans),
        ],
        compiler_params=pltpu.CompilerParams(
            collective_id=0, has_side_effects=True, vmem_limit_bytes=56 * 2**20
        ),
    )(
        grid_latent, mesh_latent, edge_sender[0], target, nbr_index,
        halo_send.reshape(1, -1), w_edge_send, w_edge_recv, b_edge[:, None], w_edge_out,
        ln_gain[:, None], w_query, w_key, w_value, w_attn_out,
    )


def solution(mesh):
    in_specs = (
        P("member", "patch"),
        P("member", "patch"),
        P("patch", None, None),
        P(None, "patch", None),
        P(),
        P(None, "patch"),
        P("patch", None, None),
        P(None, "chan"),
        P(None, "chan"),
        P("chan"),
        P("chan", None),
        P(),
        P(),
        P(),
        P(None, "chan"),
        P("chan", None),
    )
    out_specs = P("member", "patch")
    return jax.shard_map(
        per_device, mesh=mesh, in_specs=in_specs, out_specs=out_specs, check_vma=False
    )
```

```python
import functools

import jax
import jax.numpy as jnp
from jax import lax
from jax.experimental import pallas as pl
from jax.experimental.pallas import tpu as pltpu
from jax.sharding import PartitionSpec as P

HEADS = 4
BF16 = jnp.bfloat16
F32 = jnp.float32
VMEM = pltpu.VMEM
QUERY_BLOCK = 256
NODE_BLOCK = 512
ONEHOT_ROWS = 256
COUNT_ROWS = 64


def contract0(weight, operand):
    return lax.dot_general(
        weight, operand, (((0,), (0,)), ((), ())), preferred_element_type=F32
    )


def one_hot(first, rows, index_row):
    shape = (rows, index_row.shape[1])
    ids = lax.broadcasted_iota(jnp.int32, shape, 0)
    return jnp.where(ids == index_row - first, 1.0, 0.0).astype(BF16)


def column(row):
    return jnp.broadcast_to(row, (8, row.shape[1])).T[:, :1]


def pick_columns(table_ref, index_row):
    picked = None
    for first in range(0, table_ref.shape[1], ONEHOT_ROWS):
        term = jnp.dot(
            table_ref[:, first : first + ONEHOT_ROWS],
            one_hot(first, ONEHOT_ROWS, index_row),
            preferred_element_type=F32,
        )
        picked = term if picked is None else picked + term
    return picked


def kernel(
    patches, chans,
    grid_ref, mesh_ref, sender_ref, receiver_ref, edge_count_ref, nbr_ref, offer_ref,
    w_send_ref, w_recv_ref, bias_ref, w_edge_out_ref, gain_ref, w_query_ref, w_key_ref,
    w_value_ref, w_attn_out_ref,
    out_ref,
    sender_table, recv_table, send_buf, recv_buf, received, acc, sums,
    w_edge_out, w_attn_out, encoded, query, key, value, offered_acc, offered, halo, count,
    blended,
    weight_send, weight_recv, edge_send, edge_recv, sum_send, sum_recv, halo_send, halo_recv,
    blend_send, blend_recv,
):
    patch = lax.axis_index("patch")
    chan = lax.axis_index("chan")
    nodes = mesh_ref.shape[1]
    width = w_value_ref.shape[1]
    head_size = query.shape[0]
    node_blocks = nodes // NODE_BLOCK
    query_blocks = nodes // QUERY_BLOCK
    halo_rows = halo.shape[2]

    barrier = pltpu.get_barrier_semaphore()
    for off in range(1, chans):
        pl.semaphore_signal(
            barrier, inc=1, device_id={"chan": lax.rem(chan + off, chans)},
            device_id_type=pl.DeviceIdType.MESH,
        )
    for off in range(1, patches):
        pl.semaphore_signal(
            barrier, inc=1, device_id={"patch": lax.rem(patch + off, patches)},
            device_id_type=pl.DeviceIdType.MESH,
        )
    pl.semaphore_wait(barrier, chans + patches - 2)

    def to_chans(source, target, send_sems, recv_sems):
        return [
            pltpu.make_async_remote_copy(
                src_ref=source, dst_ref=target,
                send_sem=send_sems.at[off - 1], recv_sem=recv_sems.at[off - 1],
                device_id={"chan": lax.rem(chan + off, chans)},
                device_id_type=pl.DeviceIdType.MESH,
            )
            for off in range(1, chans)
        ]

    bias = column(bias_ref[...])
    gain = column(gain_ref[...])
    pending = []

    def start(copies):
        for copy in copies:
            copy.start()
        pending.extend(copies)
        return copies

    def hop(buffer, block, way, distance, sems):
        step = 1 - 2 * way
        source = chan - step * (distance - 1)
        return pltpu.make_async_remote_copy(
            src_ref=buffer.at[block, source], dst_ref=buffer.at[block, source],
            send_sem=sems[0].at[way, block, distance - 1],
            recv_sem=sems[1].at[way, block, distance - 1],
            device_id={"chan": chan + step}, device_id_type=pl.DeviceIdType.MESH,
        )

    def sends(way, distance):
        if way == 0:
            return jnp.logical_and(chan >= distance - 1, chan < chans - 1)
        return jnp.logical_and(chan + distance <= chans, chan > 0)

    def receives(way, distance):
        return chan >= distance if way == 0 else chan + distance < chans

    def hop_send(buffer, block, distance, sems):
        for way in range(2):

            @pl.when(sends(way, distance))
            def _():
                hop(buffer, block, way, distance, sems).start()

    def hop_wait(buffer, block, distance, sems):
        for way in range(2):

            @pl.when(receives(way, distance))
            def _():
                step = 1 - 2 * way
                source = chan - step * distance
                pltpu.make_async_remote_copy(
                    src_ref=buffer.at[block, source], dst_ref=buffer.at[block, source],
                    send_sem=sems[0].at[way, block, distance - 1],
                    recv_sem=sems[1].at[way, block, distance - 1],
                    device_id={"chan": chan - step}, device_id_type=pl.DeviceIdType.MESH,
                ).wait_recv()

            if distance < chans - 1:

                @pl.when(sends(way, distance + 1))
                def _():
                    hop(buffer, block, way, distance + 1, sems).start()

    def hop_tick(buffer, tick, blocks, sems):
        for distance in range(1, chans - 1):
            block = tick - 2 * (distance - 1)
            if 0 <= block < blocks:
                hop_wait(buffer, block, distance, sems)

    def hop_finish(buffer, blocks, sems):
        for block in range(blocks):
            for distance in range(1, chans):
                for way in range(2):

                    @pl.when(sends(way, distance))
                    def _():
                        hop(buffer, block, way, distance, sems).wait_send()

    sum_sems = (sum_send, sum_recv)
    blend_sems = (blend_send, blend_recv)

    edge_out_copies = start(
        to_chans(w_edge_out_ref, w_edge_out.at[chan], weight_send.at[0], weight_recv.at[0])
    )
    w_edge_out[chan] = w_edge_out_ref[...]
    w_attn_out[chan] = w_attn_out_ref[...]

    sender_table[...] = contract0(w_send_ref[...], grid_ref[...]).astype(BF16)
    offs = sorted(range(1, patches), key=lambda off: -min(off, patches - off))
    edge_copies = {}
    for off in offs:
        other = lax.rem(patch + off, patches)
        send_buf[off] = pick_columns(sender_table, sender_ref[0, pl.ds(other, 1), :]).astype(BF16)
        edge_copies[off] = pltpu.make_async_remote_copy(
            src_ref=send_buf.at[off], dst_ref=recv_buf.at[off],
            send_sem=edge_send.at[off], recv_sem=edge_recv.at[off],
            device_id={"patch": other}, device_id_type=pl.DeviceIdType.MESH,
        )
        start([edge_copies[off]])
    attn_out_copies = start(
        to_chans(w_attn_out_ref, w_attn_out.at[chan], weight_send.at[1], weight_recv.at[1])
    )
    recv_buf[0] = pick_columns(sender_table, sender_ref[0, pl.ds(patch, 1), :]).astype(BF16)

    recv_table[...] = contract0(w_recv_ref[...], mesh_ref[...]).astype(BF16)
    order = [0] + offs
    for off in order:
        band = lax.rem(patch + patches - off, patches)
        received[off] = pick_columns(recv_table, receiver_ref[band]).astype(BF16)
    for place, off in enumerate(order):
        if off:
            edge_copies[off].wait_recv()
        band = lax.rem(patch + patches - off, patches)
        receivers = receiver_ref[band]
        slots = lax.broadcasted_iota(jnp.int32, receivers.shape, 1)
        index_row = jnp.where(slots < edge_count_ref[band, patch], receivers, -1)
        summed = recv_buf[off].astype(F32) + received[off].astype(F32) + bias
        hidden = (summed / (1.0 + jnp.exp(-summed))).astype(BF16)
        for first in range(0, nodes, ONEHOT_ROWS):
            columns = slice(first, first + ONEHOT_ROWS)
            term = lax.dot_general(
                hidden, one_hot(first, ONEHOT_ROWS, index_row),
                (((1,), (1,)), ((), ())), preferred_element_type=F32,
            )
            if place:
                term += acc[:, columns]
            acc[:, columns] = term

    for block in range(node_blocks):
        sums[block, chan] = acc[:, block * NODE_BLOCK : (block + 1) * NODE_BLOCK].astype(BF16)
        hop_send(sums, block, 1, sum_sems)

    def count_block(block):
        index = nbr_ref[:, block * QUERY_BLOCK : (block + 1) * QUERY_BLOCK]
        ids = lax.broadcasted_iota(jnp.int32, (COUNT_ROWS, QUERY_BLOCK), 0)

        def body(step, carry):
            first = step * COUNT_ROWS
            here = ids + first
            total = jnp.zeros((COUNT_ROWS, QUERY_BLOCK), F32)
            for slot in range(index.shape[0]):
                total += jnp.where(here == index[slot : slot + 1, :], 1.0, 0.0)
            rows = pl.ds(pl.multiple_of(first, COUNT_ROWS), COUNT_ROWS)
            count[block, rows, :] = total.astype(BF16)
            return carry

        lax.fori_loop(0, count.shape[1] // COUNT_ROWS, body, 0)

    last_lag = max(0, 2 * (chans - 3))
    for tick in range(max(query_blocks - 1, node_blocks + last_lag)):
        if tick < query_blocks - 1:
            count_block(tick)
        hop_tick(sums, tick, node_blocks, sum_sems)

    for copy in edge_out_copies:
        copy.wait_recv()
    head = chan * width // head_size
    columns = pl.ds(pl.multiple_of(head * head_size, head_size), head_size)
    for block in range(node_blocks):
        hop_wait(sums, block, chans - 1, sum_sems)
        here = slice(block * NODE_BLOCK, (block + 1) * NODE_BLOCK)
        hidden_units = chans * w_edge_out.shape[1]
        weight = w_edge_out[...].reshape(hidden_units, -1)
        node_sum = sums[block].reshape(hidden_units, -1)
        enc = mesh_ref[:, here].astype(F32) + contract0(weight, node_sum)
        encoded[:, here] = enc
        average = jnp.mean(enc, axis=0, keepdims=True)
        centred = enc - average
        variance = jnp.mean(centred * centred, axis=0, keepdims=True)
        normed = (centred * lax.rsqrt(variance + 1e-05) * gain).astype(BF16)
        query[:, here] = contract0(w_query_ref[:, columns], normed).astype(BF16)
        block_key = contract0(w_key_ref[:, columns], normed).astype(BF16)
        block_value = contract0(w_value_ref[...], normed).astype(BF16)
        key[here, :] = block_key.T
        value[:, here] = block_value
        for side in range(2):
            hot = one_hot(block * NODE_BLOCK, NODE_BLOCK, offer_ref[0, side : side + 1, :])
            key_term = jnp.dot(block_key, hot, preferred_element_type=F32)
            value_term = jnp.dot(block_value, hot, preferred_element_type=F32)
            if block:
                key_term += offered_acc[side, :head_size]
                value_term += offered_acc[side, head_size:]
            offered_acc[side, :head_size] = key_term
            offered_acc[side, head_size:] = value_term

    halo_copies = []
    for side in range(2):
        offered[side] = offered_acc[side].astype(BF16)
        step = 1 if side == 1 else patches - 1
        halo_copies.append(
            pltpu.make_async_remote_copy(
                src_ref=offered.at[side], dst_ref=halo.at[side],
                send_sem=halo_send.at[side], recv_sem=halo_recv.at[side],
                device_id={"patch": lax.rem(patch + step, patches)},
                device_id_type=pl.DeviceIdType.MESH,
            )
        )
    start(halo_copies)
    count_block(query_blocks - 1)
    first = nodes
    for side in (1, 0):
        halo_copies[side].wait_recv()
        key[first : first + halo_rows, :] = halo[side, :head_size].T
        value[:, first : first + halo_rows] = halo[side, head_size:]
        first += halo_rows

    for block in range(query_blocks):
        here = slice(block * QUERY_BLOCK, (block + 1) * QUERY_BLOCK)
        scores = jnp.dot(key[...], query[:, here], preferred_element_type=F32)
        scores = scores * (head_size**-0.5)
        slots = count[block].astype(F32)
        scores = jnp.where(slots > 0.0, scores, -3e38)
        top = jnp.max(scores, axis=0, keepdims=True)
        weight = jnp.where(slots > 0.0, jnp.exp(scores - top), 0.0)
        total = jnp.sum(weight * slots, axis=0, keepdims=True)
        attention = (weight * (1.0 / total)).astype(BF16) * count[block]
        mixed = jnp.dot(value[...], attention, preferred_element_type=F32).astype(BF16)
        blended[block, chan] = mixed
        hop_send(blended, block, 1, blend_sems)
        hop_tick(blended, block - 1, query_blocks, blend_sems)
    for tick in range(query_blocks - 1, query_blocks + last_lag):
        hop_tick(blended, tick, query_blocks, blend_sems)

    for copy in attn_out_copies:
        copy.wait_recv()
    for block in range(query_blocks):
        hop_wait(blended, block, chans - 1, blend_sems)
        here = slice(block * QUERY_BLOCK, (block + 1) * QUERY_BLOCK)
        rows = chans * w_attn_out.shape[1]
        weight = w_attn_out[...].reshape(rows, -1)
        update = contract0(weight, blended[block].reshape(rows, -1))
        out_ref[:, here] = (encoded[:, here] + update).astype(BF16)

    for copy in pending:
        copy.wait_send()
    hop_finish(sums, node_blocks, sum_sems)
    hop_finish(blended, query_blocks, blend_sems)


def per_device(
    grid_latent,
    mesh_latent,
    edge_sender,
    edge_receiver,
    edge_count,
    nbr_index,
    halo_send,
    w_edge_send,
    w_edge_recv,
    b_edge,
    w_edge_out,
    ln_gain,
    w_query,
    w_key,
    w_value,
    w_attn_out,
):
    patches = lax.axis_size("patch")
    chans = lax.axis_size("chan")
    model_width, nodes = mesh_latent.shape
    capacity = edge_sender.shape[2]
    halo_rows = halo_send.shape[2]
    hidden = w_edge_send.shape[1]
    width = w_value.shape[1]
    head_size = model_width // HEADS
    both = head_size + width
    table_rows = nodes + 2 * halo_rows
    node_blocks = nodes // NODE_BLOCK
    query_blocks = nodes // QUERY_BLOCK
    sem = lambda *shape: pltpu.SemaphoreType.DMA(shape)
    return pl.pallas_call(
        functools.partial(kernel, patches, chans),
        out_shape=jax.ShapeDtypeStruct((model_width, nodes), BF16),
        in_specs=[pl.BlockSpec(memory_space=pltpu.SMEM if i == 4 else VMEM) for i in range(16)],
        out_specs=pl.BlockSpec(memory_space=VMEM),
        scratch_shapes=[
            VMEM((hidden, grid_latent.shape[1]), BF16),
            VMEM((hidden, nodes), BF16),
            VMEM((patches, hidden, capacity), BF16),
            VMEM((patches, hidden, capacity), BF16),
            VMEM((patches, hidden, capacity), BF16),
            VMEM((hidden, nodes), F32),
            VMEM((node_blocks, chans, hidden, NODE_BLOCK), BF16),
            VMEM((chans,) + w_edge_out.shape, BF16),
            VMEM((chans,) + w_attn_out.shape, BF16),
            VMEM((model_width, nodes), F32),
            VMEM((head_size, nodes), BF16),
            VMEM((table_rows, head_size), BF16),
            VMEM((width, table_rows), BF16),
            VMEM((2, both, halo_rows), F32),
            VMEM((2, both, halo_rows), BF16),
            VMEM((2, both, halo_rows), BF16),
            VMEM((query_blocks, table_rows, QUERY_BLOCK), BF16),
            VMEM((query_blocks, chans, width, QUERY_BLOCK), BF16),
            sem(2, chans), sem(2, chans),
            sem(patches), sem(patches),
            sem(2, node_blocks, chans), sem(2, node_blocks, chans),
            sem(2), sem(2),
            sem(2, query_blocks, chans), sem(2, query_blocks, chans),
        ],
        compiler_params=pltpu.CompilerParams(
            collective_id=0, has_side_effects=True, vmem_limit_bytes=56 * 2**20
        ),
    )(
        grid_latent, mesh_latent, edge_sender, edge_receiver, edge_count, nbr_index,
        halo_send, w_edge_send, w_edge_recv, b_edge.reshape(1, -1), w_edge_out,
        ln_gain.reshape(1, -1), w_query, w_key, w_value, w_attn_out,
    )


def solution(mesh):
    in_specs = (
        P("member", "patch"),
        P("member", "patch"),
        P("patch", None, None),
        P(None, "patch", None),
        P(),
        P(None, "patch"),
        P("patch", None, None),
        P(None, "chan"),
        P(None, "chan"),
        P("chan"),
        P("chan", None),
        P(),
        P(),
        P(),
        P(None, "chan"),
        P("chan", None),
    )
    out_specs = P("member", "patch")
    return jax.shard_map(
        per_device, mesh=mesh, in_specs=in_specs, out_specs=out_specs, check_vma=False
    )
```
